128 devices in a mesh: dp: 8 (over x, y_lo), seq: 16 (over z, y_hi, core).
Axes of the slice: x: 4, y: 4 (y_hi: 2, y_lo: 2; y = y_hi * 2 + y_lo), z: 4, core: 2. Of those that a mesh axis runs over, the one named last changes fastest.
Arguments:
- projected: bfloat16 [8, 2048, 6144], P('dp', 'seq'), may hold values from -24 to 24
- upstream: bfloat16 [8, 2048, 2048], P('dp', 'seq'), may hold values from -6 to 6
- w_out: bfloat16 [2048, 2048], replicated, may hold values from -0.125 to 0.125
- partners: int32 [16, 3], replicated, may hold values from 0 to 15, as said below
Outputs:
- grad_projected: bfloat16 [8, 2048, 6144], P('dp', 'seq')
- grad_w_out: float32 [2048, 2048], P(None, ('dp', 'seq'))
The draws below stay inside these ranges and needn't reach their ends.
Inputs may be any that keep to these rules, and one draw needn't show every extreme that they name: `partners`: split the 16 blocks into runs of 1 block; column r maps each run one to one onto the run that lies (r + 1) * 2 runs later, counted cyclically.
All inputs are finite; a program needn't handle non-finite values.
Results may differ from the reference program's by a relative error of at most 0.0064.
Values may be sent and summed in bfloat16 or wider, within the bound.
No kernel may reach another device: no remote copies, remote signals or barrier semaphores. Data moves between devices by JAX's collectives and lax.ppermute only.
A program may use at most 192 MiB of HBM per device.

```python
from functools import partial
import jax
import jax.numpy as jnp
from jax import lax

D = 2048
HD = 128
HW = 16
BLOCK = 128
RAND = 3
TOK_DEV = 128
LEN = 2048
SEQS = 8
NB = 16


def draw_projected(key, part):
    first = jax.random.fold_in(key, 0)
    width = HW * HD
    shape = (SEQS, LEN, 3 * width)
    base = jnp.clip(jax.random.normal(first, shape, jnp.float32), -4.0, 4.0)
    return base.astype(jnp.bfloat16)


def shuffled(single, count):
    return jax.random.permutation(single, count)


def draw_partners(key, part):
    per_run = TOK_DEV // BLOCK
    runs = NB // per_run
    spacing = runs // (2 * RAND + 1)
    many_keys = jax.random.split(key, RAND * runs)
    orders = jax.vmap(partial(shuffled, count=per_run))(many_keys).astype(jnp.int32).reshape(RAND, runs, per_run)
    run_ids = jnp.arange(runs, dtype=jnp.int32)
    columns = []
    for step in range(RAND):
        target = (run_ids + (step + 1) * spacing) % runs
        columns.append((target[:, None] * per_run + orders[step]).reshape(NB))
    return jnp.stack(columns, axis=1).astype(jnp.int32)


def raised(values, rng, source, target, parts, factor):
    def block_of(position):
        return (jnp.arange(values.shape[position]) // (values.shape[position] // parts)).reshape((-1,) + (1,) * (values.ndim - 1 - position))

    one_side = jax.random.permutation(rng, parts)[block_of(target)]
    other_side = (block_of(target) + parts // 2) % parts
    return jnp.where((block_of(source) == one_side) | (block_of(source) == other_side), factor * values, values)


def level_of(own_key, shape, pieces, smallest, largest):
    factor_of = 1.0
    for dim, parts in pieces:
        draws = jax.random.uniform(jax.random.fold_in(jax.random.fold_in(own_key, 6), dim), (parts,), jnp.float32, smallest / len(pieces), largest / len(pieces))
        factor_of = factor_of * jnp.repeat(jnp.exp(draws), shape[dim] // parts).reshape((-1,) + (1,) * (len(shape) - 1 - dim))
    return factor_of


def scatter_about(rng, extent, deviation, bound, shards=(), held_as=jnp.bfloat16):
    result = jax.random.normal(rng, extent, jnp.float32) * deviation
    if len(shards) > 0:
        result = level_of(rng, extent, shards, -0.22, 0.18) * result
    return jnp.clip(result, min=-bound, max=bound).astype(held_as)


def heavy_noise(rng, shape, deviation, reach, shards, heavy, kind=jnp.bfloat16):
    result = deviation * jax.random.normal(rng, shape, jnp.float32)
    if shards:
        result = result * level_of(rng, shape, shards, -0.22, 0.18)
    return jnp.clip(raised(result, jax.random.fold_in(rng, 3), *heavy), -reach, reach).astype(kind)


def setup_inputs(seed: int = 0) -> dict:
    arg_keys = jax.random.split(jax.random.key(seed), 5)
    return {
        "projected": draw_projected(jax.random.fold_in(arg_keys[4], 71), 0),
        "upstream": heavy_noise(arg_keys[1], (SEQS, LEN, D), 1.0, 6.0, ((0, 8), (1, 16)), (1, 2, 16, 2.0)),
        "w_out": scatter_about(arg_keys[2], (HW * HD, D), (HW * HD) ** -0.5, 0.125),
        "partners": draw_partners(jax.random.fold_in(arg_keys[4], 71), 0),
    }


def round_half(value):
    return lax.optimization_barrier(value.astype(jnp.bfloat16)).astype(jnp.float32)


def block_links(partners):
    block_ids = jnp.arange(NB, dtype=jnp.int32)
    chosen = jnp.any(partners[:, :, None] == block_ids[None, None, :], axis=1)
    nearby = jnp.abs(block_ids[:, None] - block_ids[None, :]) <= 1
    border = (block_ids == 0) | (block_ids == NB - 1)
    return chosen | chosen.T | nearby | border[:, None] | border[None, :]


def one_sequence(projected, upstream, w_out, links):
    width = HW * HD
    scale = HD ** -0.5
    queries = projected[:, :width].astype(jnp.float32).reshape(LEN, HW, HD)
    keys = projected[:, width:2 * width].astype(jnp.float32).reshape(LEN, HW, HD)
    values = projected[:, 2 * width:].astype(jnp.float32).reshape(LEN, HW, HD)
    out_grad_all = jnp.dot(upstream, w_out.T, preferred_element_type=jnp.float32).astype(jnp.bfloat16)

    def block_step(carry, index):
        start = (index * BLOCK).astype(jnp.int32)
        query = lax.dynamic_slice_in_dim(queries, start, BLOCK, 0)
        out_grad = lax.dynamic_slice_in_dim(out_grad_all, start, BLOCK, 0).astype(jnp.float32).reshape(BLOCK, HW, HD)
        link_row = lax.dynamic_index_in_dim(links, index.astype(jnp.int32), 0, keepdims=False)
        visible = jnp.repeat(link_row, BLOCK)[None, None, :]
        scores = jnp.einsum("qhd,khd->hqk", query, keys) * scale
        scores = jnp.where(visible, scores, -1e30)
        row_max = jnp.max(scores, axis=2, keepdims=True)
        exponent = jnp.where(visible, jnp.exp(scores - row_max), 0.0)
        total = jnp.sum(exponent, axis=2, keepdims=True)
        attended = jnp.einsum("hqk,khd->hqd", round_half(exponent), values) / total
        attended = jnp.transpose(attended, (1, 0, 2))
        probs = exponent / total
        prob_grad = jnp.einsum("qhd,khd->hqk", out_grad, values)
        delta = jnp.transpose(jnp.sum(out_grad * attended, axis=2), (1, 0))[:, :, None]
        score_grad = round_half(probs * (prob_grad - delta))
        query_grad = jnp.einsum("hqk,khd->qhd", score_grad, keys) * scale
        key_term = jnp.einsum("hqk,qhd->khd", score_grad, query) * scale
        value_term = jnp.einsum("hqk,qhd->khd", round_half(probs), out_grad)
        partial_value = jnp.concatenate([key_term.reshape(LEN, width), value_term.reshape(LEN, width)], axis=1)
        return carry + round_half(partial_value), (query_grad.reshape(BLOCK, width), attended.reshape(BLOCK, width))

    start_carry = jnp.zeros((LEN, 2 * width), jnp.float32)
    key_grads, (query_grad, attended) = lax.scan(block_step, start_carry, jnp.arange(NB, dtype=jnp.int32))
    qkv_grad = jnp.concatenate([query_grad.reshape(LEN, width), key_grads], axis=1).astype(jnp.bfloat16)
    attended_out = attended.reshape(LEN, width).astype(jnp.bfloat16)
    grad_w_out = jnp.dot(attended_out.T, upstream, preferred_element_type=jnp.float32)
    return qkv_grad, grad_w_out


def reference(projected, upstream, w_out, partners):
    links = block_links(partners)

    def each(index):
        return one_sequence(projected[index], upstream[index], w_out, links)

    grad_projected, grad_w_out = lax.map(each, jnp.arange(SEQS, dtype=jnp.int32))
    factor = (SEQS * LEN) ** -0.5
    return grad_projected, jnp.sum(grad_w_out, axis=0) * factor
```

```python
import functools
import math

import jax
import jax.numpy as jnp
from jax import lax
from jax.experimental import pallas as pl
from jax.experimental.pallas import tpu as pltpu
from jax.sharding import Mesh, PartitionSpec as P

HD = 128
BLOCK = 128
RAND = 3
SEQ = ("z1", "z0", "yh", "core")
NB = 16
SCALE = HD ** (-0.5)
VMEM_LIMIT = 48 * 1024 * 1024
EXP_SCALE = SCALE * math.log2(math.e)


def linked_blocks(block):
    if block in (0, NB - 1):
        return list(range(NB))
    seen = {block - 1, block, block + 1, 0, NB - 1}
    for step in range(RAND):
        shift = (step + 1) * (NB // (2 * RAND + 1))
        seen |= {(block + shift) % NB, (block - shift) % NB}
    return sorted(seen)


def dot(a, b, dims):
    return lax.dot_general(a, b, (dims, ((), ())), preferred_element_type=jnp.float32)


def attention_kernel(qkv, grad, d_qkv, attended, keys_t, values_t, d_keys, d_values):
    for c in range(NB):
        rows = slice(c * BLOCK, (c + 1) * BLOCK)
        keys_t[:, rows] = qkv[c, :, HD : 2 * HD].T
        values_t[:, rows] = qkv[c, :, 2 * HD :].T
    d_keys[...] = jnp.zeros_like(d_keys)
    d_values[...] = jnp.zeros_like(d_values)
    for b in range(NB):
        seen = linked_blocks(b)
        query = qkv[b, :, :HD]
        g = grad[b]
        keys = jnp.concatenate([qkv[c, :, HD : 2 * HD] for c in seen], axis=0)
        values = jnp.concatenate([qkv[c, :, 2 * HD :] for c in seen], axis=0)
        scores = dot(keys, query, ((1,), (1,)))
        prob_grad = dot(values, g, ((1,), (1,)))
        row_max = jnp.max(scores, axis=0, keepdims=True)
        weights = jnp.exp2((scores - row_max) * EXP_SCALE)
        inverse = 1.0 / jnp.sum(weights, axis=0, keepdims=True)
        v_t = jnp.concatenate([values_t[:, c * BLOCK : (c + 1) * BLOCK] for c in seen], axis=1)
        k_t = jnp.concatenate([keys_t[:, c * BLOCK : (c + 1) * BLOCK] for c in seen], axis=1)
        att = dot(v_t, weights.astype(jnp.bfloat16), ((1,), (0,))) * inverse
        attended[b] = att.astype(jnp.bfloat16)
        probs = weights * inverse
        delta = jnp.sum(probs * prob_grad, axis=0, keepdims=True)
        score_grad = (probs * (prob_grad - delta)).astype(jnp.bfloat16)
        probs = probs.astype(jnp.bfloat16)
        d_query = dot(k_t, score_grad, ((1,), (0,))) * SCALE
        d_qkv[b, :, :HD] = d_query.T.astype(jnp.bfloat16)
        key_term = dot(score_grad, query, ((1,), (0,)))
        value_term = dot(probs, g, ((1,), (0,)))
        for n, c in enumerate(seen):
            d_keys[c] += key_term[n * BLOCK : (n + 1) * BLOCK]
            d_values[c] += value_term[n * BLOCK : (n + 1) * BLOCK]
    for c in range(NB):
        d_qkv[c, :, HD : 2 * HD] = (d_keys[c] * SCALE).astype(jnp.bfloat16)
        d_qkv[c, :, 2 * HD :] = d_values[c].astype(jnp.bfloat16)


def attention(qkv, grad):
    vmem = pl.BlockSpec(memory_space=pltpu.VMEM)
    return pl.pallas_call(
        attention_kernel,
        out_shape=(
            jax.ShapeDtypeStruct((NB, BLOCK, 3 * HD), jnp.bfloat16),
            jax.ShapeDtypeStruct((NB, HD, BLOCK), jnp.bfloat16),
        ),
        in_specs=[vmem, vmem],
        out_specs=(vmem, vmem),
        scratch_shapes=[
            pltpu.VMEM((HD, NB * BLOCK), jnp.bfloat16),
            pltpu.VMEM((HD, NB * BLOCK), jnp.bfloat16),
            pltpu.VMEM((NB, BLOCK, HD), jnp.float32),
            pltpu.VMEM((NB, BLOCK, HD), jnp.float32),
        ],
        compiler_params=pltpu.CompilerParams(vmem_limit_bytes=VMEM_LIMIT),
        cost_estimate=pl.CostEstimate(flops=5_000_000_000, bytes_accessed=5_000_000, transcendentals=3_000_000),
        name="attention",
    )(qkv, grad)


def whole_call(kernel, out, name, *arrays, flops=0):
    vmem = pl.BlockSpec(memory_space=pltpu.VMEM)
    outs = out if isinstance(out, tuple) else (out,)
    moved = sum(x.size * x.dtype.itemsize for x in (*arrays, *outs))
    return pl.pallas_call(
        kernel,
        out_shape=out,
        in_specs=[vmem] * len(arrays),
        out_specs=jax.tree.map(lambda _: vmem, out),
        compiler_params=pltpu.CompilerParams(vmem_limit_bytes=VMEM_LIMIT),
        cost_estimate=pl.CostEstimate(flops=flops, bytes_accessed=moved, transcendentals=0),
        name=name,
    )(*arrays)


def pack_heads_kernel(rows, packed):
    heads = packed.shape[0]
    for h in range(heads):
        for kind in range(3):
            column = (kind * heads + h) * HD
            packed[h, :, kind * HD : (kind + 1) * HD] = rows[:, column : column + HD]


def unpack_heads_kernel(packed, rows):
    heads = packed.shape[0]
    for h in range(heads):
        for kind in range(3):
            column = (kind * heads + h) * HD
            rows[:, column : column + HD] = packed[h, :, kind * HD : (kind + 1) * HD]


def out_grad_kernel(up, w_out, grad):
    product = dot(up[...], w_out[...], ((1,), (1,)))
    for h in range(grad.shape[0]):
        grad[h] = product[:, h * HD : (h + 1) * HD].astype(jnp.bfloat16)


def out_grad_heads(up, w_out):
    tokens, width = up.shape
    step = 2 * HD
    return pl.pallas_call(
        out_grad_kernel,
        grid=(width // step,),
        out_shape=jax.ShapeDtypeStruct((width // HD, tokens, HD), jnp.bfloat16),
        in_specs=[
            pl.BlockSpec((tokens, width), lambda i: (0, 0)),
            pl.BlockSpec((step, width), lambda i: (i, 0)),
        ],
        out_specs=pl.BlockSpec((step // HD, tokens, HD), lambda i: (i, 0, 0)),
        compiler_params=pltpu.CompilerParams(vmem_limit_bytes=VMEM_LIMIT),
        cost_estimate=pl.CostEstimate(
            flops=2 * tokens * width * width, bytes_accessed=2 * width * width, transcendentals=0
        ),
        name="out_grad",
    )(up, w_out)


def pack_columns_kernel(up, packed):
    for block in range(up.shape[1] // HD):
        turned = up[:, block * HD : (block + 1) * HD].T
        for granule in range(8):
            z0, yh, core = granule // 4, granule // 2 % 2, granule % 2
            piece = turned[granule * 16 : (granule + 1) * 16]
            row = (block * 2 + yh) * 16
            for z1 in range(2):
                for yh_to in range(2):
                    packed[z1 * 8 + z0 * 4 + yh_to * 2 + core, row : row + 16, :] = piece


def tile_kernel(factor, columns, own, over_core, over_z, over_both, tile):
    blocks = range(NB)
    lhs = jnp.concatenate([columns[b] for b in blocks], axis=1)
    rhs = jnp.concatenate(
        [jnp.concatenate([part[b] for b in blocks], axis=1) for part in (own, over_core, over_z, over_both)],
        axis=0,
    )
    product = (dot(lhs, rhs, ((1,), (1,))) * factor).astype(jnp.bfloat16)
    for piece in range(tile.shape[0]):
        tile[piece] = product[piece * 16 : (piece + 1) * 16]


def combine_kernel(place, tiles, out):
    z0, core = place[0], place[1]
    for group in range(4):
        z1, yh = group // 2, group % 2
        total = tiles[group].astype(jnp.float32)
        for source in range(1, tiles.shape[0] // 4):
            total += tiles[source * 4 + group].astype(jnp.float32)
        for part in range(4):
            head = z1 * 8 + (z0 ^ (part // 2)) * 4 + yh * 2 + (core ^ (part % 2))
            start = pl.multiple_of(head * HD, HD)
            out[:, pl.ds(start, HD)] = total[:, part * HD : (part + 1) * HD]


def combine(place, tiles):
    vmem = pl.BlockSpec(memory_space=pltpu.VMEM)
    return pl.pallas_call(
        combine_kernel,
        out_shape=jax.ShapeDtypeStruct((tiles.shape[1], NB * HD), jnp.float32),
        in_specs=[pl.BlockSpec(memory_space=pltpu.SMEM), vmem],
        out_specs=vmem,
        compiler_params=pltpu.CompilerParams(vmem_limit_bytes=VMEM_LIMIT),
        name="combine",
    )(place, tiles)


def on_device(projected, upstream, w_out, partners):
    rows = projected[0]
    up = upstream[0]
    tokens = rows.shape[0]
    width = w_out.shape[0]
    heads = width // HD
    dp = lax.axis_size("dp")
    column_width = width // (dp * heads)
    factor = (tokens * heads * dp) ** (-0.5)
    shape = jax.ShapeDtypeStruct

    qkv = whole_call(pack_heads_kernel, shape((heads, tokens, 3 * HD), jnp.bfloat16), "pack_heads", rows)
    qkv = lax.all_to_all(qkv, SEQ, 0, 0, tiled=True)
    grad = lax.all_to_all(out_grad_heads(up, w_out), SEQ, 0, 0, tiled=True)
    columns = whole_call(
        pack_columns_kernel, shape((heads, width // 4, tokens), jnp.bfloat16), "pack_columns", up
    )
    columns = lax.all_to_all(columns, SEQ, 0, 0, tiled=True)

    d_qkv, attended = attention(qkv, grad)

    d_rows = lax.all_to_all(d_qkv, SEQ, 0, 0, tiled=True)
    d_rows = whole_call(unpack_heads_kernel, shape(rows.shape, jnp.bfloat16), "unpack_heads", d_rows)

    flip = [(0, 1), (1, 0)]
    over_z = lax.ppermute(attended, "z0", flip)
    over_core = lax.ppermute(attended, "core", flip)
    over_both = lax.ppermute(over_z, "core", flip)
    tile = whole_call(
        functools.partial(tile_kernel, factor),
        shape((dp * 4, column_width, 4 * HD), jnp.bfloat16),
        "tile",
        columns,
        attended,
        over_core,
        over_z,
        over_both,
        flops=2 * (width // 4) ** 2 * heads * tokens,
    )
    tile = lax.all_to_all(tile, ("dp", "z1", "yh"), 0, 0, tiled=True)
    place = jnp.stack([lax.axis_index("z0"), lax.axis_index("core")]).astype(jnp.int32)
    return d_rows[None], combine(place, tile).T


def solution(mesh):
    fine = Mesh(mesh.devices.reshape(-1, 2, 2, 2, 2), ("dp",) + SEQ)
    return jax.shard_map(
        on_device,
        mesh=fine,
        in_specs=(P("dp", SEQ, None), P("dp", SEQ, None), P(), P()),
        out_specs=(P("dp", SEQ, None), P(None, ("dp",) + SEQ)),
        check_vma=False,
    )
```

```python
import functools
import math

import jax
import jax.numpy as jnp
from jax import lax
from jax.experimental import pallas as pl
from jax.experimental.pallas import tpu as pltpu
from jax.sharding import Mesh, PartitionSpec as P

HD = 128
BLOCK = 128
RAND = 3
DP = ("x", "ylo")
SEQ = ("z1", "z0", "yh", "core")
NB = 16
SCALE = HD ** (-0.5)
VMEM_LIMIT = 48 * 1024 * 1024
EXP_SCALE = SCALE * math.log2(math.e)


def linked_blocks(block):
    if block in (0, NB - 1):
        return list(range(NB))
    seen = {block - 1, block, block + 1, 0, NB - 1}
    for step in range(RAND):
        shift = (step + 1) * (NB // (2 * RAND + 1))
        seen |= {(block + shift) % NB, (block - shift) % NB}
    return sorted(seen)


def dot(a, b, dims):
    return lax.dot_general(a, b, (dims, ((), ())), preferred_element_type=jnp.float32)


def scores_of(qkv, block):
    seen = linked_blocks(block)
    keys = jnp.concatenate([qkv[c, :, HD : 2 * HD] for c in seen], axis=0)
    return seen, dot(keys, qkv[block, :, :HD], ((1,), (1,)))


def transposed(turned, seen):
    return jnp.concatenate([turned[:, c * BLOCK : (c + 1) * BLOCK] for c in seen], axis=1)


def forward_kernel(qkv, attended, stats, values_t):
    for c in range(NB):
        values_t[:, c * BLOCK : (c + 1) * BLOCK] = qkv[c, :, 2 * HD :].T
    for b in range(NB):
        seen, scores = scores_of(qkv, b)
        row_max = jnp.max(scores, axis=0, keepdims=True)
        weights = jnp.exp2((scores - row_max) * EXP_SCALE)
        inverse = 1.0 / jnp.sum(weights, axis=0, keepdims=True)
        att = dot(transposed(values_t, seen), weights.astype(jnp.bfloat16), ((1,), (0,)))
        attended[b] = (att * inverse).astype(jnp.bfloat16)
        stats[b] = jnp.concatenate([row_max, inverse], axis=0)


def backward_kernel(qkv, stats, d_qkv, keys_t, d_keys, d_values):
    for c in range(NB):
        keys_t[:, c * BLOCK : (c + 1) * BLOCK] = qkv[c, :, HD : 2 * HD].T
    d_keys[...] = jnp.zeros_like(d_keys)
    d_values[...] = jnp.zeros_like(d_values)
    for b in range(NB):
        seen, scores = scores_of(qkv, b)
        query = qkv[b, :, :HD]
        grad = qkv[b, :, 3 * HD :]
        values = jnp.concatenate([qkv[c, :, 2 * HD : 3 * HD] for c in seen], axis=0)
        prob_grad = dot(values, grad, ((1,), (1,)))
        probs = jnp.exp2((scores - stats[b, 0:1]) * EXP_SCALE) * stats[b, 1:2]
        delta = jnp.sum(probs * prob_grad, axis=0, keepdims=True)
        score_grad = (probs * (prob_grad - delta)).astype(jnp.bfloat16)
        d_query = dot(transposed(keys_t, seen), score_grad, ((1,), (0,))) * SCALE
        d_qkv[b, :, :HD] = d_query.T.astype(jnp.bfloat16)
        key_term = dot(score_grad, query, ((1,), (0,)))
        value_term = dot(probs.astype(jnp.bfloat16), grad, ((1,), (0,)))
        for n, c in enumerate(seen):
            d_keys[c] += key_term[n * BLOCK : (n + 1) * BLOCK]
            d_values[c] += value_term[n * BLOCK : (n + 1) * BLOCK]
    for c in range(NB):
        d_qkv[c, :, HD : 2 * HD] = (d_keys[c] * SCALE).astype(jnp.bfloat16)
        d_qkv[c, :, 2 * HD :] = d_values[c].astype(jnp.bfloat16)


def whole_call(kernel, out, name, *arrays, place=None, blocks=None, scratch=(), flops=0):
    blocks = blocks or {}

    def spec(x, block=None):
        shape, index = block or (x.shape, (0,) * len(x.shape))
        return pl.BlockSpec(shape, lambda i: index)

    moved = sum(x.size * x.dtype.itemsize for x in (*arrays, *jax.tree.leaves(out)))
    scalars = () if place is None else (place,)
    return pl.pallas_call(
        kernel,
        grid=(1,),
        out_shape=out,
        in_specs=[pl.BlockSpec(memory_space=pltpu.SMEM)] * len(scalars)
        + [spec(x, blocks.get(n)) for n, x in enumerate(arrays)],
        out_specs=jax.tree.map(spec, out),
        scratch_shapes=scratch,
        compiler_params=pltpu.CompilerParams(vmem_limit_bytes=VMEM_LIMIT),
        cost_estimate=pl.CostEstimate(flops=flops, bytes_accessed=moved, transcendentals=0),
        name=name,
    )(*scalars, *arrays)


def pack_kernel(up, w_out, queries, keys, values, packed, up_t):
    step = pl.program_id(0)

    @pl.when(step == 0)
    def _():
        for block in range(up.shape[1] // HD):
            columns = slice(block * HD, (block + 1) * HD)
            up_t[columns, :] = up[:, columns].T

    grad = dot(w_out[...], up_t[...], ((1,), (0,)))
    z0 = lax.rem(step // 2, 2)
    for core in range(2):
        columns = slice(core * HD, (core + 1) * HD)
        packed[core, :, :HD] = queries[:, columns]
        packed[core, :, HD : 2 * HD] = keys[:, columns]
        packed[core, :, 2 * HD : 3 * HD] = values[:, columns]
        packed[core, :, 3 * HD : 4 * HD] = grad[columns].T.astype(jnp.bfloat16)
        for granule in range(up.shape[1] // 64):
            start = pl.multiple_of(granule // 2 * 128 + z0 * 64 + granule % 2 * 32 + core * 16, 16)
            chunk, row = granule // 8, granule % 8 * 16
            packed[core, row : row + 16, (chunk + 4) * HD : (chunk + 5) * HD] = up_t[pl.ds(start, 16), :]


def pack(rows, up, w_out):
    tokens, width = up.shape
    step = 2 * HD
    steps = width // step
    return pl.pallas_call(
        pack_kernel,
        grid=(steps,),
        out_shape=jax.ShapeDtypeStruct((width // HD, tokens, 8 * HD), jnp.bfloat16),
        in_specs=[
            pl.BlockSpec((tokens, width), lambda i: (0, 0)),
            pl.BlockSpec((step, width), lambda i: (i, 0)),
            pl.BlockSpec((tokens, step), lambda i: (0, i)),
            pl.BlockSpec((tokens, step), lambda i: (0, steps + i)),
            pl.BlockSpec((tokens, step), lambda i: (0, 2 * steps + i)),
        ],
        out_specs=pl.BlockSpec((2, tokens, 8 * HD), lambda i: (i, 0, 0)),
        scratch_shapes=[pltpu.VMEM((width, tokens), jnp.bfloat16)],
        compiler_params=pltpu.CompilerParams(vmem_limit_bytes=VMEM_LIMIT),
        cost_estimate=pl.CostEstimate(
            flops=2 * tokens * width * width, bytes_accessed=2 * width * width, transcendentals=0
        ),
        name="pack",
    )(up, w_out, rows, rows, rows)


def unpack_heads_kernel(packed, rows):
    heads = packed.shape[0]
    for h in range(heads):
        for kind in range(3):
            column = (kind * heads + h) * HD
            rows[:, column : column + HD] = packed[h, :, kind * HD : (kind + 1) * HD]


def tile_kernel(factor, place, columns, own, over_core, over_z, over_both, *outs):
    *outs, product = outs
    blocks = range(NB)
    lhs = jnp.concatenate(
        [
            jnp.concatenate([columns[b, :, chunk * HD : (chunk + 1) * HD] for b in blocks], axis=1)
            for chunk in range(4)
        ],
        axis=0,
    )
    rhs = jnp.concatenate(
        [jnp.concatenate([part[b] for b in blocks], axis=1) for part in (own, over_core, over_z, over_both)],
        axis=0,
    )
    product[...] = dot(lhs, rhs, ((1,), (1,))) * factor
    rows = outs[0].shape[0]
    for far, out in enumerate(outs):
        to = lax.rem(place[2] + far, len(outs))
        out[...] = product[pl.ds(pl.multiple_of(to * rows, rows), rows), :].astype(out.dtype)


def sum_kernel(place, *refs):
    tiles, outs, total = refs[:4], refs[4:-1], refs[-1]
    value = tiles[0][...].astype(jnp.float32)
    for tile in tiles[1:]:
        value += tile[...].astype(jnp.float32)
    total[...] = value
    rows = outs[0].shape[0]
    for far, out in enumerate(outs):
        to = place[3] ^ far
        out[...] = total[pl.ds(pl.multiple_of(to * rows, rows), rows), :]


def combine_kernel(place, *refs):
    *parts, out = refs
    for far in range(4):
        source = place[3] ^ far
        z1, yh = lax.rem(source // 2, 2), lax.rem(source, 2)
        total = parts[far][...] + parts[far + 4][...]
        for near in range(4):
            head = z1 * 8 + (place[0] ^ (near // 2)) * 4 + yh * 2 + (place[1] ^ (near % 2))
            start = pl.multiple_of(head * HD, HD)
            out[:, pl.ds(start, HD)] = total[:, near * HD : (near + 1) * HD]


def on_device(projected, upstream, w_out, partners):
    rows = projected[0]
    up = upstream[0]
    tokens = rows.shape[0]
    width = w_out.shape[0]
    heads = width // HD
    dp = lax.axis_size("x") * lax.axis_size("ylo")
    column_width = width // (dp * heads)
    factor = (tokens * heads * dp) ** (-0.5)
    shape = jax.ShapeDtypeStruct
    eight = ("ylo", "z1", "yh")
    place = jnp.stack([lax.axis_index(a) for a in ("z0", "core", "x", eight)]).astype(jnp.int32)

    packed = lax.all_to_all(pack(rows, up, w_out), SEQ, 0, 0, tiled=True)
    attended, stats = whole_call(
        forward_kernel,
        (shape((NB, HD, BLOCK), jnp.bfloat16), shape((NB, 2, BLOCK), jnp.float32)),
        "forward",
        packed,
        blocks={0: ((NB, BLOCK, 3 * HD), (0, 0, 0))},
        scratch=[pltpu.VMEM((HD, NB * BLOCK), jnp.bfloat16)],
        flops=2_000_000_000,
    )
    flip = [(0, 1), (1, 0)]
    over_z = lax.ppermute(attended, "z0", flip)
    over_core = lax.ppermute(attended, "core", flip)
    d_qkv = whole_call(
        backward_kernel,
        shape((NB, BLOCK, 3 * HD), jnp.bfloat16),
        "backward",
        packed,
        stats,
        blocks={0: ((NB, BLOCK, 4 * HD), (0, 0, 0))},
        scratch=[
            pltpu.VMEM((HD, NB * BLOCK), jnp.bfloat16),
            pltpu.VMEM((NB, BLOCK, HD), jnp.float32),
            pltpu.VMEM((NB, BLOCK, HD), jnp.float32),
        ],
        flops=4_000_000_000,
    )
    d_qkv, over_z, over_core = lax.optimization_barrier((d_qkv, over_z, over_core))
    over_both = lax.ppermute(over_z, "core", flip)
    d_rows = lax.all_to_all(d_qkv, SEQ, 0, 0, tiled=True)

    tiles = whole_call(
        functools.partial(tile_kernel, factor),
        (shape((width // 16, 4 * HD), jnp.bfloat16),) * 4,
        "tile",
        packed,
        attended,
        over_core,
        over_z,
        over_both,
        place=place,
        blocks={0: ((NB, BLOCK, 4 * HD), (0, 0, 1))},
        scratch=[pltpu.VMEM((width // 4, 4 * HD), jnp.float32)],
        flops=2 * (width // 4) ** 2 * heads * tokens,
    )
    tiles = [tiles[0]] + [
        lax.ppermute(tiles[far], "x", [(i, (i + far) % 4) for i in range(4)]) for far in range(1, 4)
    ]
    parts = whole_call(
        sum_kernel,
        (shape((column_width, 4 * HD), jnp.float32),) * 8,
        "sum_tiles",
        *tiles,
        place=place,
        scratch=[pltpu.VMEM((width // 16, 4 * HD), jnp.float32)],
    )
    parts = [parts[0]] + [lax.ppermute(parts[far], eight, [(i, i ^ far) for i in range(8)]) for far in range(1, 8)]
    grad_w_out = whole_call(
        combine_kernel, shape((column_width, width), jnp.float32), "combine", *parts, place=place
    )
    d_rows = whole_call(unpack_heads_kernel, shape(rows.shape, jnp.bfloat16), "unpack_heads", d_rows)
    return d_rows[None], grad_w_out.T


def solution(mesh):
    fine = Mesh(mesh.devices.reshape(4, 2, 2, 2, 2, 2), DP + SEQ)
    return jax.shard_map(
        on_device,
        mesh=fine,
        in_specs=(P(DP, SEQ, None), P(DP, SEQ, None), P(), P()),
        out_specs=(P(DP, SEQ, None), P(None, DP + SEQ)),
        check_vma=False,
    )
```

```python
import functools
import math

import jax
import jax.numpy as jnp
from jax import lax
from jax.experimental import pallas as pl
from jax.experimental.pallas import tpu as pltpu
from jax.sharding import Mesh, PartitionSpec as P

HD = 128
BLOCK = 128
RAND = 3
DP = ("x", "ylo")
SEQ = ("z1", "z0", "yh", "core")
NB = 16
SCALE = HD ** (-0.5)
VMEM_LIMIT = 48 * 1024 * 1024
EXP_SCALE = SCALE * math.log2(math.e)


def linked_blocks(block):
    if block in (0, NB - 1):
        return list(range(NB))
    seen = {block - 1, block, block + 1, 0, NB - 1}
    for step in range(RAND):
        shift = (step + 1) * (NB // (2 * RAND + 1))
        seen |= {(block + shift) % NB, (block - shift) % NB}
    return sorted(seen)


def dot(a, b, dims):
    return lax.dot_general(a, b, (dims, ((), ())), preferred_element_type=jnp.float32)


def scores_of(qkv, block):
    seen = linked_blocks(block)
    keys = jnp.concatenate([qkv[c, :, HD : 2 * HD] for c in seen], axis=0)
    return seen, dot(keys, qkv[block, :, :HD], ((1,), (1,)))


def transposed(turned, seen):
    return jnp.concatenate([turned[:, c * BLOCK : (c + 1) * BLOCK] for c in seen], axis=1)


def forward_kernel(qkv, attended, stats, values_t):
    for c in range(NB):
        values_t[:, c * BLOCK : (c + 1) * BLOCK] = qkv[c, :, 2 * HD :].T
    for b in range(NB):
        seen, scores = scores_of(qkv, b)
        row_max = jnp.max(scores, axis=0, keepdims=True)
        weights = jnp.exp2((scores - row_max) * EXP_SCALE)
        inverse = 1.0 / jnp.sum(weights, axis=0, keepdims=True)
        att = dot(transposed(values_t, seen), weights.astype(jnp.bfloat16), ((1,), (0,)))
        attended[b] = (att * inverse).astype(jnp.bfloat16)
        stats[b] = jnp.concatenate([row_max, inverse], axis=0)


def backward_kernel(qkv, stats, d_qkv, keys_t, d_keys, d_values):
    for c in range(NB):
        keys_t[:, c * BLOCK : (c + 1) * BLOCK] = qkv[c, :, HD : 2 * HD].T
    d_keys[...] = jnp.zeros_like(d_keys)
    d_values[...] = jnp.zeros_like(d_values)
    for b in range(NB):
        seen, scores = scores_of(qkv, b)
        query = qkv[b, :, :HD]
        grad = qkv[b, :, 3 * HD :]
        values = jnp.concatenate([qkv[c, :, 2 * HD : 3 * HD] for c in seen], axis=0)
        prob_grad = dot(values, grad, ((1,), (1,)))
        probs = jnp.exp2((scores - stats[b, 0:1]) * EXP_SCALE) * stats[b, 1:2]
        delta = jnp.sum(probs * prob_grad, axis=0, keepdims=True)
        score_grad = (probs * (prob_grad - delta)).astype(jnp.bfloat16)
        d_query = dot(transposed(keys_t, seen), score_grad, ((1,), (0,))) * SCALE
        d_qkv[b, :, :HD] = d_query.T.astype(jnp.bfloat16)
        key_term = dot(score_grad, query, ((1,), (0,)))
        value_term = dot(probs.astype(jnp.bfloat16), grad, ((1,), (0,)))
        for n, c in enumerate(seen):
            d_keys[c] += key_term[n * BLOCK : (n + 1) * BLOCK]
            d_values[c] += value_term[n * BLOCK : (n + 1) * BLOCK]
    for c in range(NB):
        d_qkv[c, :, HD : 2 * HD] = (d_keys[c] * SCALE).astype(jnp.bfloat16)
        d_qkv[c, :, 2 * HD :] = d_values[c].astype(jnp.bfloat16)


def whole_call(kernel, out, name, *arrays, place=None, blocks=None, scratch=(), flops=0):
    blocks = blocks or {}

    def spec(x, block=None):
        shape, index = block or (x.shape, (0,) * len(x.shape))
        return pl.BlockSpec(shape, lambda i: index)

    moved = sum(x.size * x.dtype.itemsize for x in (*arrays, *jax.tree.leaves(out)))
    scalars = () if place is None else (place,)
    return pl.pallas_call(
        kernel,
        grid=(1,),
        out_shape=out,
        in_specs=[pl.BlockSpec(memory_space=pltpu.SMEM)] * len(scalars)
        + [spec(x, blocks.get(n)) for n, x in enumerate(arrays)],
        out_specs=jax.tree.map(spec, out),
        scratch_shapes=scratch,
        compiler_params=pltpu.CompilerParams(vmem_limit_bytes=VMEM_LIMIT),
        cost_estimate=pl.CostEstimate(flops=flops, bytes_accessed=moved, transcendentals=0),
        name=name,
    )(*scalars, *arrays)


def pack_kernel(up, w_out, queries, keys, values, packed, up_t):
    step = pl.program_id(0)

    @pl.when(step == 0)
    def _():
        for block in range(up.shape[1] // HD):
            columns = slice(block * HD, (block + 1) * HD)
            up_t[columns, :] = up[:, columns].T

    grad = dot(w_out[...], up_t[...], ((1,), (0,)))
    z0 = lax.rem(step, 2)
    for h in range(packed.shape[0]):
        columns = slice(h * HD, (h + 1) * HD)
        packed[h, :, :HD] = queries[:, columns]
        packed[h, :, HD : 2 * HD] = keys[:, columns]
        packed[h, :, 2 * HD : 3 * HD] = values[:, columns]
        packed[h, :, 3 * HD : 4 * HD] = grad[columns].T.astype(jnp.bfloat16)
        for granule in range(up.shape[1] // 64):
            start = pl.multiple_of(granule // 2 * 128 + z0 * 64 + granule % 2 * 32 + h % 2 * 16, 16)
            chunk, row = granule // 8, granule % 8 * 16
            packed[h, row : row + 16, (chunk + 4) * HD : (chunk + 5) * HD] = up_t[pl.ds(start, 16), :]


def pack(rows, up, w_out):
    tokens, width = up.shape
    step = 4 * HD
    steps = width // step
    return pl.pallas_call(
        pack_kernel,
        grid=(steps,),
        out_shape=jax.ShapeDtypeStruct((width // HD, tokens, 8 * HD), jnp.bfloat16),
        in_specs=[
            pl.BlockSpec((tokens, width), lambda i: (0, 0)),
            pl.BlockSpec((step, width), lambda i: (i, 0)),
            pl.BlockSpec((tokens, step), lambda i: (0, i)),
            pl.BlockSpec((tokens, step), lambda i: (0, steps + i)),
            pl.BlockSpec((tokens, step), lambda i: (0, 2 * steps + i)),
        ],
        out_specs=pl.BlockSpec((step // HD, tokens, 8 * HD), lambda i: (i, 0, 0)),
        scratch_shapes=[pltpu.VMEM((width, tokens), jnp.bfloat16)],
        compiler_params=pltpu.CompilerParams(vmem_limit_bytes=60 * 1024 * 1024),
        cost_estimate=pl.CostEstimate(
            flops=2 * tokens * width * width, bytes_accessed=2 * width * width, transcendentals=0
        ),
        name="pack",
    )(up, w_out, rows, rows, rows)


def unpack_heads_kernel(packed, rows):
    heads = packed.shape[0]
    for h in range(heads):
        for kind in range(3):
            column = (kind * heads + h) * HD
            rows[:, column : column + HD] = packed[h, :, kind * HD : (kind + 1) * HD]


def tile_kernel(factor, place, columns, own, over_core, over_z, over_both, *outs):
    *outs, product = outs
    blocks = range(NB)
    lhs = jnp.concatenate(
        [
            jnp.concatenate([columns[b, :, chunk * HD : (chunk + 1) * HD] for b in blocks], axis=1)
            for chunk in range(4)
        ],
        axis=0,
    )
    rhs = jnp.concatenate(
        [jnp.concatenate([part[b] for b in blocks], axis=1) for part in (own, over_core, over_z, over_both)],
        axis=0,
    )
    product[...] = dot(lhs, rhs, ((1,), (1,))) * factor
    rows = outs[0].shape[0]
    for far, out in enumerate(outs):
        to = lax.rem(place[2] + far, len(outs))
        out[...] = product[pl.ds(pl.multiple_of(to * rows, rows), rows), :].astype(out.dtype)


def sum_kernel(place, *refs):
    tiles, outs, total = refs[:4], refs[4:-1], refs[-1]
    value = tiles[0][...].astype(jnp.float32)
    for tile in tiles[1:]:
        value += tile[...].astype(jnp.float32)
    total[...] = value
    rows = outs[0].shape[0]
    for far, out in enumerate(outs):
        to = place[3] ^ far
        out[...] = total[pl.ds(pl.multiple_of(to * rows, rows), rows), :]


def combine_kernel(place, *refs):
    *parts, out = refs
    for far in range(4):
        source = place[3] ^ far
        z1, yh = lax.rem(source // 2, 2), lax.rem(source, 2)
        total = parts[far][...] + parts[far + 4][...]
        for near in range(4):
            head = z1 * 8 + (place[0] ^ (near // 2)) * 4 + yh * 2 + (place[1] ^ (near % 2))
            start = pl.multiple_of(head * HD, HD)
            out[:, pl.ds(start, HD)] = total[:, near * HD : (near + 1) * HD]


def on_device(projected, upstream, w_out, partners):
    rows = projected[0]
    up = upstream[0]
    tokens = rows.shape[0]
    width = w_out.shape[0]
    heads = width // HD
    dp = lax.axis_size("x") * lax.axis_size("ylo")
    column_width = width // (dp * heads)
    factor = (tokens * heads * dp) ** (-0.5)
    shape = jax.ShapeDtypeStruct
    eight = ("ylo", "z1", "yh")
    place = jnp.stack([lax.axis_index(a) for a in ("z0", "core", "x", eight)]).astype(jnp.int32)

    packed = lax.all_to_all(pack(rows, up, w_out), SEQ, 0, 0, tiled=True)
    attended, stats = whole_call(
        forward_kernel,
        (shape((NB, HD, BLOCK), jnp.bfloat16), shape((NB, 2, BLOCK), jnp.float32)),
        "forward",
        packed,
        blocks={0: ((NB, BLOCK, 3 * HD), (0, 0, 0))},
        scratch=[pltpu.VMEM((HD, NB * BLOCK), jnp.bfloat16)],
        flops=2_000_000_000,
    )
    flip = [(0, 1), (1, 0)]
    over_z = lax.ppermute(attended, "z0", flip)
    over_core = lax.ppermute(attended, "core", flip)
    d_qkv = whole_call(
        backward_kernel,
        shape((NB, BLOCK, 3 * HD), jnp.bfloat16),
        "backward",
        packed,
        stats,
        blocks={0: ((NB, BLOCK, 4 * HD), (0, 0, 0))},
        scratch=[
            pltpu.VMEM((HD, NB * BLOCK), jnp.bfloat16),
            pltpu.VMEM((NB, BLOCK, HD), jnp.float32),
            pltpu.VMEM((NB, BLOCK, HD), jnp.float32),
        ],
        flops=4_000_000_000,
    )
    d_qkv, over_z, over_core = lax.optimization_barrier((d_qkv, over_z, over_core))
    over_both = lax.ppermute(over_z, "core", flip)
    d_rows = lax.all_to_all(d_qkv, SEQ, 0, 0, tiled=True)

    tiles = whole_call(
        functools.partial(tile_kernel, factor),
        (shape((width // 16, 4 * HD), jnp.bfloat16),) * 4,
        "tile",
        packed,
        attended,
        over_core,
        over_z,
        over_both,
        place=place,
        blocks={0: ((NB, BLOCK, 4 * HD), (0, 0, 1))},
        scratch=[pltpu.VMEM((width // 4, 4 * HD), jnp.float32)],
        flops=2 * (width // 4) ** 2 * heads * tokens,
    )
    tiles = [tiles[0]] + [
        lax.ppermute(tiles[far], "x", [(i, (i + far) % 4) for i in range(4)]) for far in range(1, 4)
    ]
    parts = whole_call(
        sum_kernel,
        (shape((column_width, 4 * HD), jnp.float32),) * 8,
        "sum_tiles",
        *tiles,
        place=place,
        scratch=[pltpu.VMEM((width // 16, 4 * HD), jnp.float32)],
    )
    parts = [parts[0]] + [lax.ppermute(parts[far], eight, [(i, i ^ far) for i in range(8)]) for far in range(1, 8)]
    d_rows = whole_call(unpack_heads_kernel, shape(rows.shape, jnp.bfloat16), "unpack_heads", d_rows)
    parts, d_rows = lax.optimization_barrier((parts, d_rows))
    grad_w_out = whole_call(
        combine_kernel, shape((column_width, width), jnp.float32), "combine", *parts, place=place
    )
    return d_rows[None], grad_w_out.T


def solution(mesh):
    fine = Mesh(mesh.devices.reshape(4, 2, 2, 2, 2, 2), DP + SEQ)
    return jax.shard_map(
        on_device,
        mesh=fine,
        in_specs=(P(DP, SEQ, None), P(DP, SEQ, None), P(), P()),
        out_specs=(P(DP, SEQ, None), P(None, DP + SEQ)),
        check_vma=False,
    )
```

```python
import functools
import math

import jax
import jax.numpy as jnp
from jax import lax
from jax.experimental import pallas as pl
from jax.experimental.pallas import tpu as pltpu
from jax.sharding import Mesh, PartitionSpec as P

HD = 128
BLOCK = 128
RAND = 3
DP = ("x", "ylo")
SEQ = ("z1", "z0", "yh", "core")
NB = 16
SCALE = HD ** (-0.5)
VMEM_LIMIT = 48 * 1024 * 1024
EXP_SCALE = SCALE * math.log2(math.e)


def linked_blocks(block):
    if block in (0, NB - 1):
        return list(range(NB))
    seen = {block - 1, block, block + 1, 0, NB - 1}
    for step in range(RAND):
        shift = (step + 1) * (NB // (2 * RAND + 1))
        seen |= {(block + shift) % NB, (block - shift) % NB}
    return sorted(seen)


def dot(a, b, dims):
    return lax.dot_general(a, b, (dims, ((), ())), preferred_element_type=jnp.float32)


def scores_of(qkv, block):
    seen = linked_blocks(block)
    keys = jnp.concatenate([qkv[c, :, HD : 2 * HD] for c in seen], axis=0)
    return seen, dot(keys, qkv[block, :, :HD], ((1,), (1,)))


def transposed(turned, seen):
    return jnp.concatenate([turned[:, c * BLOCK : (c + 1) * BLOCK] for c in seen], axis=1)


def halves(first, second):
    first, second = first.astype(jnp.float32), second.astype(jnp.float32)
    half = HD // 2
    return (
        jnp.concatenate([first[:, :half], second[:, :half]], axis=1),
        jnp.concatenate([first[:, half:], second[:, half:]], axis=1),
    )


def forward_kernel(place, qkv, near, far, stats, values_t):
    even = None
    first = place[3] // 2 % 2 == 0
    for c in range(NB):
        values_t[:, c * BLOCK : (c + 1) * BLOCK] = qkv[c, :, 2 * HD :].T
    for b in range(NB):
        seen, scores = scores_of(qkv, b)
        row_max = jnp.max(scores, axis=0, keepdims=True)
        weights = jnp.exp2((scores - row_max) * EXP_SCALE)
        inverse = 1.0 / jnp.sum(weights, axis=0, keepdims=True)
        att = dot(transposed(values_t, seen), weights.astype(jnp.bfloat16), ((1,), (0,)))
        att = att * inverse
        if b % 2 == 0:
            even = att
        else:
            low, high = halves(even, att)
            near[b // 2] = jnp.where(first, low, high).astype(jnp.bfloat16)
            far[b // 2] = jnp.where(first, high, low).astype(jnp.bfloat16)
        stats[b] = jnp.concatenate([row_max, inverse], axis=0)


def backward_kernel(qkv, stats, d_qkv, keys_t, d_keys, d_values):
    for c in range(NB):
        keys_t[:, c * BLOCK : (c + 1) * BLOCK] = qkv[c, :, HD : 2 * HD].T
    d_keys[...] = jnp.zeros_like(d_keys)
    d_values[...] = jnp.zeros_like(d_values)
    for b in range(NB):
        seen, scores = scores_of(qkv, b)
        query = qkv[b, :, :HD]
        grad = qkv[b, :, 3 * HD :]
        values = jnp.concatenate([qkv[c, :, 2 * HD : 3 * HD] for c in seen], axis=0)
        prob_grad = dot(values, grad, ((1,), (1,)))
        probs = jnp.exp2((scores - stats[b, 0:1]) * EXP_SCALE) * stats[b, 1:2]
        delta = jnp.sum(probs * prob_grad, axis=0, keepdims=True)
        score_grad = (probs * (prob_grad - delta)).astype(jnp.bfloat16)
        d_query = dot(transposed(keys_t, seen), score_grad, ((1,), (0,))) * SCALE
        d_qkv[b, :, :HD] = d_query.T.astype(jnp.bfloat16)
        key_term = dot(score_grad, query, ((1,), (0,)))
        value_term = dot(probs.astype(jnp.bfloat16), grad, ((1,), (0,)))
        for n, c in enumerate(seen):
            d_keys[c] += key_term[n * BLOCK : (n + 1) * BLOCK]
            d_values[c] += value_term[n * BLOCK : (n + 1) * BLOCK]
    for c in range(NB):
        d_qkv[c, :, HD : 2 * HD] = (d_keys[c] * SCALE).astype(jnp.bfloat16)
        d_qkv[c, :, 2 * HD :] = d_values[c].astype(jnp.bfloat16)


def whole_call(kernel, out, name, *arrays, place=None, blocks=None, scratch=(), flops=0):
    blocks = blocks or {}

    def spec(x, block=None):
        shape, index = block or (x.shape, (0,) * len(x.shape))
        return pl.BlockSpec(shape, lambda i: index)

    moved = sum(x.size * x.dtype.itemsize for x in (*arrays, *jax.tree.leaves(out)))
    scalars = () if place is None else (place,)
    return pl.pallas_call(
        kernel,
        grid=(1,),
        out_shape=out,
        in_specs=[pl.BlockSpec(memory_space=pltpu.SMEM)] * len(scalars)
        + [spec(x, blocks.get(n)) for n, x in enumerate(arrays)],
        out_specs=jax.tree.map(spec, out),
        scratch_shapes=scratch,
        compiler_params=pltpu.CompilerParams(vmem_limit_bytes=VMEM_LIMIT),
        cost_estimate=pl.CostEstimate(flops=flops, bytes_accessed=moved, transcendentals=0),
        name=name,
    )(*scalars, *arrays)


def pack_kernel(up, w_out, queries, keys, values, packed, up_t):
    step = pl.program_id(0)

    @pl.when(step == 0)
    def _():
        for block in range(up.shape[1] // HD):
            columns = slice(block * HD, (block + 1) * HD)
            up_t[columns, :] = up[:, columns].T

    grad = dot(w_out[...], up_t[...], ((1,), (0,)))
    z1, z0 = step // 2, lax.rem(step, 2)
    for h in range(packed.shape[0]):
        columns = slice(h * HD, (h + 1) * HD)
        packed[h, :, :HD] = queries[:, columns]
        packed[h, :, HD : 2 * HD] = keys[:, columns]
        packed[h, :, 2 * HD : 3 * HD] = values[:, columns]
        packed[h, :, 3 * HD : 4 * HD] = grad[columns].T.astype(jnp.bfloat16)
    for core in range(2):
        chunks = []
        for chunk in range(4):
            starts = [
                chunk * 512 + n // 4 * 256 + z1 * 128 + n // 2 % 2 * 64 + n % 2 * 32 + core * 16 for n in range(8)
            ]
            chunks.append(jnp.concatenate([up_t[pl.ds(pl.multiple_of(n, 16), 16), :] for n in starts], axis=0))
        for side in range(2):
            low, high = halves(chunks[2 * side], chunks[2 * side + 1])
            piece = jnp.where(z0 == 0, low, high).astype(jnp.bfloat16)
            for h in (core, core + 2):
                packed[h, :, (side + 4) * HD : (side + 5) * HD] = piece


def pack(rows, up, w_out):
    tokens, width = up.shape
    step = 4 * HD
    steps = width // step
    return pl.pallas_call(
        pack_kernel,
        grid=(steps,),
        out_shape=jax.ShapeDtypeStruct((width // HD, tokens, 6 * HD), jnp.bfloat16),
        in_specs=[
            pl.BlockSpec((tokens, width), lambda i: (0, 0)),
            pl.BlockSpec((step, width), lambda i: (i, 0)),
            pl.BlockSpec((tokens, step), lambda i: (0, i)),
            pl.BlockSpec((tokens, step), lambda i: (0, steps + i)),
            pl.BlockSpec((tokens, step), lambda i: (0, 2 * steps + i)),
        ],
        out_specs=pl.BlockSpec((step // HD, tokens, 6 * HD), lambda i: (i, 0, 0)),
        scratch_shapes=[pltpu.VMEM((width, tokens), jnp.bfloat16)],
        compiler_params=pltpu.CompilerParams(vmem_limit_bytes=60 * 1024 * 1024),
        cost_estimate=pl.CostEstimate(
            flops=2 * tokens * width * width, bytes_accessed=2 * width * width, transcendentals=0
        ),
        name="pack",
    )(up, w_out, rows, rows, rows)


def unpack_heads_kernel(packed, rows):
    heads = packed.shape[0]
    for h in range(heads):
        for kind in range(3):
            column = (kind * heads + h) * HD
            rows[:, column : column + HD] = packed[h, :, kind * HD : (kind + 1) * HD]


def tile_kernel(factor, place, columns, *refs):
    parts, outs, product = refs[:8], refs[8:-1], refs[-1]
    lhs = []
    for side in range(2):
        lanes = slice(side * HD, (side + 1) * HD)
        pairs = [halves(columns[2 * m, :, lanes], columns[2 * m + 1, :, lanes]) for m in range(NB // 2)]
        for half in range(2):
            lhs.append(jnp.concatenate([p[half].astype(jnp.bfloat16) for p in pairs], axis=1))
    lhs = jnp.concatenate(lhs, axis=0)
    rhs = jnp.concatenate(
        [jnp.concatenate([part[m] for m in range(NB // 2)], axis=1) for part in parts],
        axis=0,
    )
    product[...] = dot(lhs, rhs, ((1,), (1,))) * factor
    rows = outs[0].shape[0]
    for far, out in enumerate(outs):
        to = lax.rem(place[2] + far, len(outs))
        out[...] = product[pl.ds(pl.multiple_of(to * rows, rows), rows), :].astype(out.dtype)


def sum_kernel(*refs):
    *tiles, out = refs
    value = tiles[0][...].astype(jnp.float32)
    for tile in tiles[1:]:
        value += tile[...].astype(jnp.float32)
    rows = out.shape[1]
    for to in range(out.shape[0]):
        out[to] = value[to * rows : (to + 1) * rows].astype(out.dtype)


def combine_kernel(place, parts, out):
    for yh in range(2):
        for head_z0 in range(2):
            for far in range(4):
                far_z1, far_core = far // 2, far % 2
                total = None
                for ylo in range(2):
                    for sender_z0 in range(2):
                        lane = ((head_z0 ^ sender_z0) * 4 + far_z1 * 2 + far_core) * HD
                        piece = parts[ylo * 4 + sender_z0 * 2 + yh, :, lane : lane + HD].astype(jnp.float32)
                        total = piece if total is None else total + piece
                head = (place[0] ^ far_z1) * 8 + head_z0 * 4 + yh * 2 + (place[1] ^ far_core)
                out[:, pl.ds(pl.multiple_of(head * HD, HD), HD)] = total


def on_device(projected, upstream, w_out, partners):
    rows = projected[0]
    up = upstream[0]
    tokens = rows.shape[0]
    width = w_out.shape[0]
    heads = width // HD
    dp = lax.axis_size("x") * lax.axis_size("ylo")
    column_width = width // (dp * heads)
    factor = (tokens * heads * dp) ** (-0.5)
    shape = jax.ShapeDtypeStruct
    eight = ("ylo", "z0", "yh")
    place = jnp.stack([lax.axis_index(a) for a in ("z1", "core", "x", eight)]).astype(jnp.int32)

    packed = lax.all_to_all(pack(rows, up, w_out), SEQ, 0, 0, tiled=True)
    near, far, stats = whole_call(
        forward_kernel,
        (shape((NB // 2, HD, BLOCK), jnp.bfloat16),) * 2 + (shape((NB, 2, BLOCK), jnp.float32),),
        "forward",
        packed,
        place=place,
        blocks={0: ((NB, BLOCK, 3 * HD), (0, 0, 0))},
        scratch=[pltpu.VMEM((HD, NB * BLOCK), jnp.bfloat16)],
        flops=2_000_000_000,
    )
    flip = [(0, 1), (1, 0)]
    over_z = [
        lax.ppermute(near, "z1", flip),
        lax.ppermute(far, "z0", flip),
        lax.ppermute(far, ("z1", "z0"), [(i, 3 - i) for i in range(4)]),
    ]
    over_core = lax.ppermute(near, "core", flip)
    d_qkv = whole_call(
        backward_kernel,
        shape((NB, BLOCK, 3 * HD), jnp.bfloat16),
        "backward",
        packed,
        stats,
        blocks={0: ((NB, BLOCK, 4 * HD), (0, 0, 0))},
        scratch=[
            pltpu.VMEM((HD, NB * BLOCK), jnp.bfloat16),
            pltpu.VMEM((NB, BLOCK, HD), jnp.float32),
            pltpu.VMEM((NB, BLOCK, HD), jnp.float32),
        ],
        flops=4_000_000_000,
    )
    d_qkv, over_z, over_core = lax.optimization_barrier((d_qkv, over_z, over_core))
    parts = [near, over_core]
    for part in over_z:
        parts += [part, lax.ppermute(part, "core", flip)]
    d_rows = lax.all_to_all(d_qkv, SEQ, 0, 0, tiled=True)

    tiles = whole_call(
        functools.partial(tile_kernel, factor),
        (shape((width // 16, 8 * HD), jnp.bfloat16),) * 4,
        "tile",
        packed,
        *parts,
        place=place,
        blocks={0: ((NB, BLOCK, 2 * HD), (0, 0, 2))},
        scratch=[pltpu.VMEM((width // 4, 8 * HD), jnp.float32)],
        flops=2 * (width // 4) ** 2 * heads * tokens,
    )
    tiles = [tiles[0]] + [
        lax.ppermute(tiles[far], "x", [(i, (i + far) % 4) for i in range(4)]) for far in range(1, 4)
    ]
    parts = whole_call(sum_kernel, shape((8, column_width, 8 * HD), jnp.bfloat16), "sum_tiles", *tiles)
    parts, d_rows = lax.optimization_barrier((parts, d_rows))
    parts = lax.all_to_all(parts, eight, 0, 0, tiled=True)
    d_rows = whole_call(unpack_heads_kernel, shape(rows.shape, jnp.bfloat16), "unpack_heads", d_rows)
    grad_w_out = whole_call(
        combine_kernel, shape((column_width, width), jnp.float32), "combine", parts, place=place
    )
    return d_rows[None], grad_w_out.T


def solution(mesh):
    fine = Mesh(mesh.devices.reshape(4, 2, 2, 2, 2, 2), DP + SEQ)
    return jax.shard_map(
        on_device,
        mesh=fine,
        in_specs=(P(DP, SEQ, None), P(DP, SEQ, None), P(), P()),
        out_specs=(P(DP, SEQ, None), P(None, DP + SEQ)),
        check_vma=False,
    )
```

```python
import functools
import math

import jax
import jax.numpy as jnp
from jax import lax
from jax.experimental import pallas as pl
from jax.experimental.pallas import tpu as pltpu
from jax.sharding import Mesh, PartitionSpec as P

HD = 128
BLOCK = 128
RAND = 3
DP = ("x", "ylo")
SEQ = ("z1", "z0", "yh", "core")
NB = 16
SCALE = HD ** (-0.5)
VMEM_LIMIT = 48 * 1024 * 1024
EXP_SCALE = SCALE * math.log2(math.e)


def linked_blocks(block):
    if block in (0, NB - 1):
        return list(range(NB))
    seen = {block - 1, block, block + 1, 0, NB - 1}
    for step in range(RAND):
        shift = (step + 1) * (NB // (2 * RAND + 1))
        seen |= {(block + shift) % NB, (block - shift) % NB}
    return sorted(seen)


def dot(a, b, dims):
    return lax.dot_general(a, b, (dims, ((), ())), preferred_element_type=jnp.float32)


def scores_of(qkv, block):
    seen = linked_blocks(block)
    keys = jnp.concatenate([qkv[c, :, HD : 2 * HD] for c in seen], axis=0)
    return seen, dot(keys, qkv[block, :, :HD], ((1,), (1,)))


def transposed(turned, seen):
    return jnp.concatenate([turned[:, c * BLOCK : (c + 1) * BLOCK] for c in seen], axis=1)


def halves(first, second):
    first, second = first.astype(jnp.float32), second.astype(jnp.float32)
    half = HD // 2
    return (
        jnp.concatenate([first[:, :half], second[:, :half]], axis=1),
        jnp.concatenate([first[:, half:], second[:, half:]], axis=1),
    )


def forward_kernel(place, qkv, near, far, stats, values_t):
    even = None
    first = place[3] // 2 % 2 == 0
    for c in range(NB):
        values_t[:, c * BLOCK : (c + 1) * BLOCK] = qkv[c, :, 2 * HD :].T
    for b in range(NB):
        seen, scores = scores_of(qkv, b)
        row_max = jnp.max(scores, axis=0, keepdims=True)
        weights = jnp.exp2((scores - row_max) * EXP_SCALE)
        inverse = 1.0 / jnp.sum(weights, axis=0, keepdims=True)
        att = dot(transposed(values_t, seen), weights.astype(jnp.bfloat16), ((1,), (0,)))
        att = att * inverse
        if b % 2 == 0:
            even = att
        else:
            low, high = halves(even, att)
            near[b // 2] = jnp.where(first, low, high).astype(jnp.bfloat16)
            far[b // 2] = jnp.where(first, high, low).astype(jnp.bfloat16)
        stats[b] = jnp.concatenate([row_max, inverse], axis=0)


def backward_kernel(qkv, stats, d_qkv, keys_t, d_keys, d_values):
    for c in range(NB):
        keys_t[:, c * BLOCK : (c + 1) * BLOCK] = qkv[c, :, HD : 2 * HD].T
    d_keys[...] = jnp.zeros_like(d_keys)
    d_values[...] = jnp.zeros_like(d_values)
    for b in range(NB):
        seen, scores = scores_of(qkv, b)
        query = qkv[b, :, :HD]
        grad = qkv[b, :, 3 * HD :]
        values = jnp.concatenate([qkv[c, :, 2 * HD : 3 * HD] for c in seen], axis=0)
        prob_grad = dot(values, grad, ((1,), (1,)))
        probs = jnp.exp2((scores - stats[b, 0:1]) * EXP_SCALE) * stats[b, 1:2]
        delta = jnp.sum(probs * prob_grad, axis=0, keepdims=True)
        score_grad = (probs * (prob_grad - delta)).astype(jnp.bfloat16)
        d_query = dot(transposed(keys_t, seen), score_grad, ((1,), (0,))) * SCALE
        d_qkv[b, :, :HD] = d_query.T.astype(jnp.bfloat16)
        key_term = dot(score_grad, query, ((1,), (0,)))
        value_term = dot(probs.astype(jnp.bfloat16), grad, ((1,), (0,)))
        for n, c in enumerate(seen):
            d_keys[c] += key_term[n * BLOCK : (n + 1) * BLOCK]
            d_values[c] += value_term[n * BLOCK : (n + 1) * BLOCK]
    for c in range(NB):
        d_qkv[c, :, HD : 2 * HD] = (d_keys[c] * SCALE).astype(jnp.bfloat16)
        d_qkv[c, :, 2 * HD :] = d_values[c].astype(jnp.bfloat16)


def whole_call(kernel, out, name, *arrays, place=None, blocks=None, scratch=(), flops=0):
    blocks = blocks or {}

    def spec(x, block=None):
        shape, index = block or (x.shape, (0,) * len(x.shape))
        return pl.BlockSpec(shape, lambda i: index)

    moved = sum(x.size * x.dtype.itemsize for x in (*arrays, *jax.tree.leaves(out)))
    scalars = () if place is None else (place,)
    return pl.pallas_call(
        kernel,
        grid=(1,),
        out_shape=out,
        in_specs=[pl.BlockSpec(memory_space=pltpu.SMEM)] * len(scalars)
        + [spec(x, blocks.get(n)) for n, x in enumerate(arrays)],
        out_specs=jax.tree.map(spec, out),
        scratch_shapes=scratch,
        compiler_params=pltpu.CompilerParams(vmem_limit_bytes=VMEM_LIMIT),
        cost_estimate=pl.CostEstimate(flops=flops, bytes_accessed=moved, transcendentals=0),
        name=name,
    )(*scalars, *arrays)


def after_kernel(*refs):
    pass


def after(value, *others):
    anywhere = pl.BlockSpec(memory_space=pl.ANY)
    return pl.pallas_call(
        after_kernel,
        out_shape=jax.ShapeDtypeStruct(value.shape, value.dtype),
        in_specs=[anywhere] * (1 + len(others)),
        out_specs=anywhere,
        input_output_aliases={0: 0},
        name="after",
    )(value, *others)


def pack_kernel(up, w_out, queries, keys, values, packed, up_t):
    step = pl.program_id(0)

    @pl.when(step == 0)
    def _():
        for block in range(up.shape[1] // HD):
            columns = slice(block * HD, (block + 1) * HD)
            up_t[columns, :] = up[:, columns].T

    grad = dot(w_out[...], up_t[...], ((1,), (0,)))
    z1, z0 = step // 2, lax.rem(step, 2)
    for h in range(packed.shape[0]):
        columns = slice(h * HD, (h + 1) * HD)
        packed[h, :, :HD] = queries[:, columns]
        packed[h, :, HD : 2 * HD] = keys[:, columns]
        packed[h, :, 2 * HD : 3 * HD] = values[:, columns]
        packed[h, :, 3 * HD : 4 * HD] = grad[columns].T.astype(jnp.bfloat16)
    for core in range(2):
        chunks = []
        for chunk in range(4):
            starts = [
                chunk * 512 + n // 4 * 256 + z1 * 128 + n // 2 % 2 * 64 + n % 2 * 32 + core * 16 for n in range(8)
            ]
            chunks.append(jnp.concatenate([up_t[pl.ds(pl.multiple_of(n, 16), 16), :] for n in starts], axis=0))
        for side in range(2):
            low, high = halves(chunks[2 * side], chunks[2 * side + 1])
            piece = jnp.where(z0 == 0, low, high).astype(jnp.bfloat16)
            for h in (core, core + 2):
                packed[h, :, (side + 4) * HD : (side + 5) * HD] = piece


def pack(rows, up, w_out):
    tokens, width = up.shape
    step = 4 * HD
    steps = width // step
    return pl.pallas_call(
        pack_kernel,
        grid=(steps,),
        out_shape=jax.ShapeDtypeStruct((width // HD, tokens, 6 * HD), jnp.bfloat16),
        in_specs=[
            pl.BlockSpec((tokens, width), lambda i: (0, 0)),
            pl.BlockSpec((step, width), lambda i: (i, 0)),
            pl.BlockSpec((tokens, step), lambda i: (0, i)),
            pl.BlockSpec((tokens, step), lambda i: (0, steps + i)),
            pl.BlockSpec((tokens, step), lambda i: (0, 2 * steps + i)),
        ],
        out_specs=pl.BlockSpec((step // HD, tokens, 6 * HD), lambda i: (i, 0, 0)),
        scratch_shapes=[pltpu.VMEM((width, tokens), jnp.bfloat16)],
        compiler_params=pltpu.CompilerParams(vmem_limit_bytes=60 * 1024 * 1024),
        cost_estimate=pl.CostEstimate(
            flops=2 * tokens * width * width, bytes_accessed=2 * width * width, transcendentals=0
        ),
        name="pack",
    )(up, w_out, rows, rows, rows)


def unpack_heads_kernel(packed, rows):
    heads = packed.shape[0]
    for h in range(heads):
        for kind in range(3):
            column = (kind * heads + h) * HD
            rows[:, column : column + HD] = packed[h, :, kind * HD : (kind + 1) * HD]


def tile_kernel(factor, place, columns, *refs):
    parts, outs, product = refs[:8], refs[8:-1], refs[-1]
    lhs = []
    for side in range(2):
        lanes = slice(side * HD, (side + 1) * HD)
        pairs = [halves(columns[2 * m, :, lanes], columns[2 * m + 1, :, lanes]) for m in range(NB // 2)]
        for half in range(2):
            lhs.append(jnp.concatenate([p[half].astype(jnp.bfloat16) for p in pairs], axis=1))
    lhs = jnp.concatenate(lhs, axis=0)
    rhs = jnp.concatenate(
        [jnp.concatenate([part[m] for m in range(NB // 2)], axis=1) for part in parts],
        axis=0,
    )
    product[...] = dot(lhs, rhs, ((1,), (1,))) * factor
    rows = outs[0].shape[0]
    for far, out in enumerate(outs):
        to = lax.rem(place[2] + far, len(outs))
        out[...] = product[pl.ds(pl.multiple_of(to * rows, rows), rows), :].astype(out.dtype)


def sum_kernel(*refs):
    *tiles, out = refs
    value = tiles[0][...].astype(jnp.float32)
    for tile in tiles[1:]:
        value += tile[...].astype(jnp.float32)
    rows = out.shape[1]
    for to in range(out.shape[0]):
        out[to] = value[to * rows : (to + 1) * rows].astype(out.dtype)


def combine_kernel(place, parts, out):
    for yh in range(2):
        for head_z0 in range(2):
            for far in range(4):
                far_z1, far_core = far // 2, far % 2
                total = None
                for ylo in range(2):
                    for sender_z0 in range(2):
                        lane = ((head_z0 ^ sender_z0) * 4 + far_z1 * 2 + far_core) * HD
                        piece = parts[ylo * 4 + sender_z0 * 2 + yh, :, lane : lane + HD].astype(jnp.float32)
                        total = piece if total is None else total + piece
                head = (place[0] ^ far_z1) * 8 + head_z0 * 4 + yh * 2 + (place[1] ^ far_core)
                out[:, pl.ds(pl.multiple_of(head * HD, HD), HD)] = total


def on_device(projected, upstream, w_out, partners):
    rows = projected[0]
    up = upstream[0]
    tokens = rows.shape[0]
    width = w_out.shape[0]
    heads = width // HD
    dp = lax.axis_size("x") * lax.axis_size("ylo")
    column_width = width // (dp * heads)
    factor = (tokens * heads * dp) ** (-0.5)
    shape = jax.ShapeDtypeStruct
    eight = ("ylo", "z0", "yh")
    place = jnp.stack([lax.axis_index(a) for a in ("z1", "core", "x", eight)]).astype(jnp.int32)

    packed = lax.all_to_all(pack(rows, up, w_out), SEQ, 0, 0, tiled=True)
    near, far, stats = whole_call(
        forward_kernel,
        (shape((NB // 2, HD, BLOCK), jnp.bfloat16),) * 2 + (shape((NB, 2, BLOCK), jnp.float32),),
        "forward",
        packed,
        place=place,
        blocks={0: ((NB, BLOCK, 3 * HD), (0, 0, 0))},
        scratch=[pltpu.VMEM((HD, NB * BLOCK), jnp.bfloat16)],
        flops=2_000_000_000,
    )
    flip = [(0, 1), (1, 0)]
    over_z = [
        lax.ppermute(near, "z1", flip),
        lax.ppermute(far, "z0", flip),
        lax.ppermute(far, ("z1", "z0"), [(i, 3 - i) for i in range(4)]),
    ]
    over_core = lax.ppermute(near, "core", flip)
    d_qkv = whole_call(
        backward_kernel,
        shape((NB, BLOCK, 3 * HD), jnp.bfloat16),
        "backward",
        packed,
        stats,
        blocks={0: ((NB, BLOCK, 4 * HD), (0, 0, 0))},
        scratch=[
            pltpu.VMEM((HD, NB * BLOCK), jnp.bfloat16),
            pltpu.VMEM((NB, BLOCK, HD), jnp.float32),
            pltpu.VMEM((NB, BLOCK, HD), jnp.float32),
        ],
        flops=4_000_000_000,
    )
    d_qkv = after(d_qkv, *over_z, over_core)
    parts = [near, over_core]
    for part in over_z:
        parts += [part, lax.ppermute(part, "core", flip)]
    d_rows = lax.all_to_all(d_qkv, SEQ, 0, 0, tiled=True)

    tiles = whole_call(
        functools.partial(tile_kernel, factor),
        (shape((width // 16, 8 * HD), jnp.bfloat16),) * 4,
        "tile",
        packed,
        *parts,
        place=place,
        blocks={0: ((NB, BLOCK, 2 * HD), (0, 0, 2))},
        scratch=[pltpu.VMEM((width // 4, 8 * HD), jnp.float32)],
        flops=2 * (width // 4) ** 2 * heads * tokens,
    )
    tiles = [tiles[0]] + [
        lax.ppermute(tiles[far], "x", [(i, (i + far) % 4) for i in range(4)]) for far in range(1, 4)
    ]
    parts = whole_call(sum_kernel, shape((8, column_width, 8 * HD), jnp.bfloat16), "sum_tiles", *tiles)
    parts, d_rows = lax.optimization_barrier((parts, d_rows))
    parts = lax.all_to_all(parts, eight, 0, 0, tiled=True)
    d_rows = whole_call(unpack_heads_kernel, shape(rows.shape, jnp.bfloat16), "unpack_heads", d_rows)
    grad_w_out = whole_call(
        combine_kernel, shape((column_width, width), jnp.float32), "combine", parts, place=place
    )
    return d_rows[None], grad_w_out.T


def solution(mesh):
    fine = Mesh(mesh.devices.reshape(4, 2, 2, 2, 2, 2), DP + SEQ)
    return jax.shard_map(
        on_device,
        mesh=fine,
        in_specs=(P(DP, SEQ, None), P(DP, SEQ, None), P(), P()),
        out_specs=(P(DP, SEQ, None), P(None, DP + SEQ)),
        check_vma=False,
    )
```
